32 devices in a mesh: lat: 8 (over z, core), row: 4 (over y, x).
Axes of the slice: x: 2, y: 2, z: 4, core: 2. Of those that a mesh axis runs over, the one named last changes fastest.
Arguments:
- inputs: bfloat16 [256, 3584], P('row', 'lat'), may hold values from -6 to 6
- encoder: bfloat16 [5376, 3584], P(('lat', 'row')), may hold values from -0.09375 to 0.09375
- latent_bias: float32 [5376], P(('lat', 'row')), may hold values from -3 to 3
- decoder: bfloat16 [5376, 3584], P(('lat', 'row')), may hold values from -0.49099025 to 0.49099025
- center_bias: float32 [3584], P('lat'), may hold values from -3 to 3
Outputs:
- encoder_grad: bfloat16 [5376, 3584], P(('lat', 'row'))
- decoder_grad: bfloat16 [5376, 3584], P(('lat', 'row'))
- bias_grad: float32 [5376], P(('lat', 'row'))
- center_grad: float32 [3584], P(('lat', 'row'))
The draws below stay inside these ranges and needn't reach their ends.
All inputs are finite; a program needn't handle non-finite values.
Results may differ from the reference program's by a relative error of at most 0.005.
Values may be sent and summed in bfloat16 or wider, within the bound.
No kernel may reach another device: no remote copies, remote signals or barrier semaphores. Data moves between devices by JAX's collectives and lax.ppermute only.
A program may use at most 64 MiB of HBM per device.

```python
import math
import jax
import jax.numpy as jnp
from jax import lax

D = 3584
ROWS = 256
LATENTS = 5376


def draw_decoder(key, part):
    key = jax.random.fold_in(key, 7)
    key_rows, key_cols, key_base = jax.random.split(key, 3)
    row_scale = jnp.exp(jax.random.uniform(key_rows, (LATENTS, 1), jnp.float32, math.log(0.3), math.log(3.0)))
    col_scale = jnp.exp(jax.random.uniform(key_cols, (1, D), jnp.float32, math.log(0.3), math.log(3.0)))
    base = jnp.clip(jax.random.normal(key_base, (LATENTS, D), jnp.float32), -4.0, 4.0)
    return (base * row_scale * col_scale * LATENTS ** (-0.5)).astype(jnp.bfloat16)


def shard_levels(own_key, extent, shards, least, largest):
    gain, own = 1.0, jax.random.fold_in(own_key, 6)
    for axis_at, shards_of in shards:
        heights = jnp.exp(jax.random.uniform(jax.random.fold_in(own, axis_at), (shards_of,), jnp.float32, least / len(shards), largest / len(shards)))
        gain = gain * jnp.repeat(heights, extent[axis_at] // shards_of).reshape([-1 if axis == axis_at else 1 for axis in range(len(extent))])
    return gain


def normal_values(rng, extent, deviation, reach, shards=(), held_as=jnp.bfloat16):
    factor_of = shard_levels(rng, extent, shards, -0.22, 0.18) if shards else 1.0
    result = jax.random.normal(rng, extent, jnp.float32) * deviation * factor_of
    return jnp.minimum(jnp.maximum(result, -reach), reach).astype(held_as)


def setup_inputs(seed: int = 0) -> dict:
    key_of = jax.random.split(jax.random.key(seed), 6)
    inputs = normal_values(key_of[0], (ROWS, D), 1.0, 6.0, ((0, 4), (1, 8)))
    encoder = normal_values(key_of[1], (LATENTS, D), D ** -0.5, 0.09375, ((0, 32),))
    latent_bias = normal_values(key_of[2], (LATENTS,), 0.5, 3.0, ((0, 32),), jnp.float32)
    decoder = draw_decoder(jax.random.fold_in(key_of[5], 71), 0)
    center_bias = normal_values(key_of[4], (D,), 0.5, 3.0, ((0, 8),), jnp.float32)
    return dict(inputs=inputs, encoder=encoder, latent_bias=latent_bias, decoder=decoder, center_bias=center_bias)


sparsity_weight = 1.0

def reference(inputs, encoder, latent_bias, decoder, center_bias):
    centered = (inputs.astype(jnp.float32) - center_bias).astype(jnp.bfloat16)
    preact = lax.dot_general(centered, encoder, (((1,), (1,)), ((), ())), preferred_element_type=jnp.float32) + latent_bias
    latents = (jax.nn.softplus(4.0 * preact) / 4.0).astype(jnp.bfloat16)
    recon = jnp.dot(latents, decoder, preferred_element_type=jnp.float32) + center_bias
    error = recon - inputs.astype(jnp.float32)
    error_half = error.astype(jnp.bfloat16)
    row_norm = jnp.sqrt(lax.optimization_barrier(jnp.sum(jnp.square(decoder.astype(jnp.float32)), axis=1)) + 1e-06)
    grad_latent = lax.dot_general(error_half, decoder, (((1,), (1,)), ((), ())), preferred_element_type=jnp.float32) + sparsity_weight * row_norm
    grad_pre = (grad_latent * jax.nn.sigmoid(4.0 * preact)).astype(jnp.bfloat16)
    encoder_grad = lax.dot_general(grad_pre, centered, (((0,), (0,)), ((), ())), preferred_element_type=jnp.float32).astype(jnp.bfloat16)
    latent_total = lax.optimization_barrier(jnp.sum(latents.astype(jnp.float32), axis=0))
    decoder_term = lax.dot_general(latents, error_half, (((0,), (0,)), ((), ())), preferred_element_type=jnp.float32)
    decoder_grad = (decoder_term + sparsity_weight * latent_total[:, None] * decoder.astype(jnp.float32) / row_norm[:, None]).astype(jnp.bfloat16)
    bias_grad = lax.optimization_barrier(jnp.sum(grad_pre.astype(jnp.float32), axis=0))
    center_grad = lax.optimization_barrier(jnp.sum(error, axis=0)) - jnp.dot(bias_grad, encoder.astype(jnp.float32), precision=lax.Precision.HIGHEST)
    return (encoder_grad, decoder_grad, bias_grad, center_grad)
```

```python
import jax
import jax.numpy as jnp
from jax import lax
from jax.sharding import PartitionSpec as P

sparsity_weight = 1.0
AXES = ("lat", "row")
CHUNKS = 2
f32 = jnp.float32
bf16 = jnp.bfloat16


def bits_below(n):
    return [1 << k for k in range(n.bit_length() - 1)]


class Grid:
    def __init__(self, mesh):
        self.lats, self.rows = mesh.shape["lat"], mesh.shape["row"]
        self.size = self.lats * self.rows
        self.core = self.rows
        self.row_bits = bits_below(self.rows)
        self.chip_bits = [2 * self.rows * b for b in bits_below(self.lats // 2)]
        self.chips = self.lats // 2

    def stream_of(self, i):
        parity = (i // self.core) % 2
        for b in self.row_bits + self.chip_bits:
            parity = parity ^ ((i // b) % 2)
        return parity

    def orders(self, bits):
        return list(zip(bits, bits[::-1]))

    def swap_core(self, v):
        return lax.ppermute(v, AXES, [(i, i ^ self.core) for i in range(self.size)])

    def step(self, v, pair):
        target = [i ^ self.core ^ pair[self.stream_of(i)] for i in range(self.size)]
        return lax.ppermute(v, AXES, list(enumerate(target)))


def on_device(grid, inputs, encoder, latent_bias, decoder, center_bias):
    me = lax.axis_index("lat") * grid.rows + lax.axis_index("row")
    core = (me // grid.core) % 2
    stream = grid.stream_of(me)
    chip = me // (2 * grid.core)
    nl, width = encoder.shape
    half, block = inputs.shape[0] // 2, 2 * inputs.shape[1]
    part = half // CHUNKS

    encoder_all = jnp.concatenate([encoder, grid.swap_core(encoder)], axis=0)
    decoder_all = jnp.concatenate([decoder, grid.swap_core(decoder)], axis=0)
    bias_all = jnp.concatenate([latent_bias, grid.swap_core(latent_bias)], axis=0)
    decoder_wide = decoder_all.astype(f32)
    norm_all = jnp.sqrt(jnp.sum(jnp.square(decoder_wide), axis=1) + 1e-06)

    shifted = inputs.astype(f32) - center_bias
    mine = jnp.where(stream == 0, shifted[:half], shifted[half:])
    other = jnp.where(stream == 0, shifted[half:], shifted[:half])
    theirs = grid.swap_core(other)
    shifted = jnp.where(
        core == 0,
        jnp.concatenate([mine, theirs], axis=1),
        jnp.concatenate([theirs, mine], axis=1),
    )

    def gather_columns(v):
        held = [v]
        for b in grid.chip_bits[::-1]:
            held = [held, [grid.step(u, (b, b)) for u in held]]
            held = held[0] + held[1]
        masks = [0]
        for b in bits_below(grid.chips)[::-1]:
            masks = masks + [m ^ b for m in masks]
        held = [u for _, u in sorted(zip(masks, held), key=lambda t: t[0])]
        for b in bits_below(grid.chips):
            flip = (chip // b) % 2 == 1
            held = [jnp.where(flip, held[k ^ b], held[k]) for k in range(len(held))]
        return jnp.concatenate(held, axis=1)

    def gather_rows(v):
        for pair in grid.orders(grid.row_bits):
            v = jnp.concatenate([v, grid.step(v, pair)], axis=0)
        return v

    def scatter_rows(v):
        for pair in grid.orders(grid.row_bits)[::-1]:
            n = v.shape[0] // 2
            v = v[:n] + grid.step(v[n:].astype(bf16), pair).astype(f32)
        return v

    def sum_chips(v):
        for pair in grid.orders(grid.chip_bits):
            v = v + grid.step(v.astype(bf16), pair).astype(f32)
        return v

    centered, latents, errors, grad_pres = [], [], [], []
    column_sum = 0.0
    blocks = gather_columns(shifted.astype(bf16))
    for k in range(CHUNKS):
        rows = slice(k * part, (k + 1) * part)
        cent = gather_rows(blocks[rows])
        preact = (
            lax.dot_general(cent, encoder_all, (((1,), (1,)), ((), ())), preferred_element_type=f32)
            + bias_all
        )
        lats = (jax.nn.softplus(4.0 * preact) / 4.0).astype(bf16)
        recon = jnp.dot(lats, decoder_all, preferred_element_type=f32)
        own = scatter_rows(recon)
        zeros = jnp.zeros((part, block), f32)
        placed = jnp.concatenate(
            [jnp.where(chip == p, shifted[rows], zeros) for p in range(grid.chips)], axis=1
        )
        error = sum_chips(own - placed)
        column_sum = column_sum + jnp.sum(error, axis=0)
        err = gather_rows(error.astype(bf16))
        grad_latent = (
            lax.dot_general(err, decoder_all, (((1,), (1,)), ((), ())), preferred_element_type=f32)
            + sparsity_weight * norm_all
        )
        grad_pre = (grad_latent * jax.nn.sigmoid(4.0 * preact)).astype(bf16)
        centered += [cent, grid.swap_core(cent)]
        latents += [lats[:, :nl], grid.swap_core(lats[:, nl:])]
        errors += [err, grid.swap_core(err)]
        grad_pres += [grad_pre]

    bias_part = sum(jnp.sum(g.astype(f32), axis=0) for g in grad_pres)
    terms = column_sum * (1.0 / grid.chips) - jnp.dot(
        bias_part, encoder_all.astype(f32), precision=lax.Precision.HIGHEST
    )
    left = (terms + grid.swap_core(terms)).reshape(1, width)

    def halve(left, b):
        n = left.shape[1] // 2
        upper = (me // b) % 2 == 1
        kept = jnp.where(upper, left[:, n:], left[:, :n])
        sent = jnp.where(upper, left[:, :n], left[:, n:])
        return kept + grid.step(sent, (b, b))

    for b in grid.chip_bits[::-1]:
        left = halve(left, b)
    left = left.reshape(2, width // grid.chips // 2)
    for b in grid.row_bits[::-1]:
        left = halve(left, b)
    center_grad = jnp.where(core == 0, left[0], left[1])

    pres = []
    for g in grad_pres:
        pres += [g[:, :nl], grid.swap_core(g[:, nl:])]
    centered, latents = jnp.concatenate(centered), jnp.concatenate(latents)
    errors, pres = jnp.concatenate(errors), jnp.concatenate(pres)
    latent_total = jnp.sum(latents.astype(f32), axis=0)
    bias_grad = jnp.sum(pres.astype(f32), axis=0)
    scale = sparsity_weight * latent_total / norm_all[:nl]
    decoder_grad = (
        lax.dot_general(latents, errors, (((0,), (0,)), ((), ())), preferred_element_type=f32)
        + scale[:, None] * decoder.astype(f32)
    ).astype(bf16)
    encoder_grad = lax.dot_general(
        pres, centered, (((0,), (0,)), ((), ())), preferred_element_type=f32
    ).astype(bf16)
    return (encoder_grad, decoder_grad, bias_grad, center_grad)


def solution(mesh):
    grid = Grid(mesh)
    in_specs = (P("row", "lat"), P(AXES, None), P(AXES), P(AXES, None), P("lat"))
    out_specs = (P(AXES, None), P(AXES, None), P(AXES), P(AXES))

    def device_function(*args):
        return on_device(grid, *args)

    return jax.shard_map(
        device_function, mesh=mesh, in_specs=in_specs, out_specs=out_specs, check_vma=False
    )
```

```python
import jax
import jax.numpy as jnp
from jax import lax
from jax.sharding import PartitionSpec as P

sparsity_weight = 1.0
AXES = ("lat", "row")
CHUNKS = 2
f32 = jnp.float32
bf16 = jnp.bfloat16


def bits_below(n):
    return [1 << k for k in range(n.bit_length() - 1)]


class Grid:
    def __init__(self, mesh):
        self.lats, self.rows = mesh.shape["lat"], mesh.shape["row"]
        self.size = self.lats * self.rows
        self.core = self.rows
        self.row_bits = bits_below(self.rows)
        self.chip_bits = [2 * self.rows * b for b in bits_below(self.lats // 2)]
        self.chips = self.lats // 2

    def stream_of(self, i):
        parity = (i // self.core) % 2
        for b in self.row_bits + self.chip_bits:
            parity = parity ^ ((i // b) % 2)
        return parity

    def orders(self, bits):
        return list(zip(bits, bits[::-1]))

    def swap_core(self, v):
        return lax.ppermute(v, AXES, [(i, i ^ self.core) for i in range(self.size)])

    def step(self, v, pair):
        target = [i ^ self.core ^ pair[self.stream_of(i)] for i in range(self.size)]
        return lax.ppermute(v, AXES, list(enumerate(target)))


def dot_rows(v, w):
    return lax.dot_general(v, w, (((1,), (1,)), ((), ())), preferred_element_type=f32)


def on_device(grid, inputs, encoder, latent_bias, decoder, center_bias):
    me = lax.axis_index("lat") * grid.rows + lax.axis_index("row")
    core = (me // grid.core) % 2
    stream = grid.stream_of(me)
    chip = me // (2 * grid.core)
    nl, width = encoder.shape
    half, block = inputs.shape[0] // 2, 2 * inputs.shape[1]
    part = half // CHUNKS

    encoders = [encoder, grid.swap_core(encoder)]
    decoders = [decoder, grid.swap_core(decoder)]
    biases = [latent_bias, grid.swap_core(latent_bias)]
    norms = [jnp.sqrt(jnp.sum(jnp.square(d.astype(f32)), axis=1) + 1e-06) for d in decoders]

    def side_by_side(mine, theirs, axis):
        return jnp.where(
            core == 0,
            jnp.concatenate([mine, theirs], axis=axis),
            jnp.concatenate([theirs, mine], axis=axis),
        )

    raw = side_by_side(inputs, grid.swap_core(inputs), 1)
    center = side_by_side(center_bias, grid.swap_core(center_bias), 0)
    shifted = jnp.where(stream == 0, raw[:half], raw[half:]).astype(f32) - center

    def gather_columns(v):
        held = [v]
        for b in grid.chip_bits[::-1]:
            held = held + [grid.step(u, (b, b)) for u in held]
        masks = [0]
        for b in bits_below(grid.chips)[::-1]:
            masks = masks + [m ^ b for m in masks]
        held = [u for _, u in sorted(zip(masks, held), key=lambda t: t[0])]
        for b in bits_below(grid.chips):
            flip = (chip // b) % 2 == 1
            held = [jnp.where(flip, held[k ^ b], held[k]) for k in range(len(held))]
        return jnp.concatenate(held, axis=1)

    orders = grid.orders(grid.row_bits)

    def gather_rows(v):
        for pair in orders[:-1]:
            v = jnp.concatenate([v, grid.step(v, pair)], axis=0)
        return [v, grid.step(v, orders[-1])]

    def scatter_rows(near, far):
        v = near + grid.step(far, orders[-1]).astype(f32)
        for pair in orders[:-1][::-1]:
            n = v.shape[0] // 2
            v = v[:n] + grid.step(v[n:].astype(bf16), pair).astype(f32)
        return v

    def sum_chips(v):
        for pair in grid.orders(grid.chip_bits):
            v = v + grid.step(v.astype(bf16), pair).astype(f32)
        return v

    columns = 0.0
    blocks = gather_columns(shifted.astype(bf16))
    parts = [slice(k * part, (k + 1) * part) for k in range(CHUNKS)]
    centered = [gather_rows(blocks[rows]) for rows in parts]
    latents, sigs, errors = [], [], []

    def forward(x):
        scaled = [4.0 * (dot_rows(x, e) + b) for e, b in zip(encoders, biases)]
        sigs.append([jax.nn.sigmoid(v) for v in scaled])
        lats = [(jax.nn.softplus(v) / 4.0).astype(bf16) for v in scaled]
        latents.append(lats)
        return sum(jnp.dot(l, d, preferred_element_type=f32) for l, d in zip(lats, decoders))

    for rows, (near, far) in zip(parts, centered):
        near, far = forward(near), forward(far).astype(bf16)
        own = scatter_rows(near, far)
        zeros = jnp.zeros((part, block), f32)
        placed = jnp.concatenate(
            [jnp.where(chip == p, shifted[rows], zeros) for p in range(grid.chips)], axis=1
        )
        error = sum_chips(own - placed)
        columns = columns + jnp.sum(error, axis=0, keepdims=True)
        errors += gather_rows(error.astype(bf16))
    centered = [c for pair in centered for c in pair]
    pres = []
    for err, sig in zip(errors, sigs):
        grads = [dot_rows(err, d) + sparsity_weight * n for d, n in zip(decoders, norms)]
        pres.append([(g * v).astype(bf16) for g, v in zip(grads, sig)])
    centered, latents, errors, pres, columns = lax.optimization_barrier(
        (centered, latents, errors, pres, columns)
    )

    terms = (1.0 / grid.chips) * columns
    for side, enc in enumerate(encoders):
        bias = sum(jnp.sum(p[side].astype(f32), axis=0) for p in pres)
        terms = terms - jnp.dot(bias, enc.astype(f32), precision=lax.Precision.HIGHEST)
    left = terms + grid.swap_core(terms)

    def halve(left, b):
        n = left.shape[1] // 2
        upper = (me // b) % 2 == 1
        kept = jnp.where(upper, left[:, n:], left[:, :n])
        sent = jnp.where(upper, left[:, :n], left[:, n:])
        return kept + grid.step(sent, (b, b))

    def all_rows(mine, theirs):
        return jnp.concatenate([*mine, grid.swap_core(jnp.concatenate(theirs, axis=0))], axis=0)

    latents = all_rows([l[0] for l in latents], [l[1] for l in latents])
    pres = all_rows([p[0] for p in pres], [p[1] for p in pres])
    errors = all_rows(errors, errors)
    centered = all_rows(centered, centered)
    latent_total = jnp.sum(latents.astype(f32), axis=0)
    scale = (sparsity_weight * latent_total / norms[0])[:, None]

    def over_rows(u, v):
        return lax.dot_general(u, v, (((0,), (0,)), ((), ())), preferred_element_type=f32)

    for k, b in enumerate((grid.row_bits + grid.chip_bits)[::-1]):
        if k == len(grid.chip_bits):
            left = left.reshape(2, width // grid.chips // 2)
        if k == 2:
            left, decoder_grad = lax.optimization_barrier((left, decoder_grad))
        if k == 3:
            left, encoder_grad = lax.optimization_barrier((left, encoder_grad))
        left = halve(left, b)
        if k == 0:
            left, latents, errors = lax.optimization_barrier((left, latents, errors))
            decoder_grad = over_rows(latents, errors) + scale * decoder.astype(f32)
            decoder_grad = decoder_grad.astype(bf16)
        if k == 1:
            left, pres, centered = lax.optimization_barrier((left, pres, centered))
            bias_grad = jnp.sum(pres.astype(f32), axis=0)
            encoder_grad = over_rows(pres, centered).astype(bf16)
    center_grad = jnp.where(core == 0, left[0], left[1])
    return (encoder_grad, decoder_grad, bias_grad, center_grad)


def solution(mesh):
    grid = Grid(mesh)
    in_specs = (P("row", "lat"), P(AXES, None), P(AXES), P(AXES, None), P("lat"))
    out_specs = (P(AXES, None), P(AXES, None), P(AXES), P(AXES))

    def device_function(*args):
        return on_device(grid, *args)

    return jax.shard_map(
        device_function, mesh=mesh, in_specs=in_specs, out_specs=out_specs, check_vma=False
    )
```

```python
import jax
import jax.numpy as jnp
from jax import lax
from jax.sharding import PartitionSpec as P

sparsity_weight = 1.0
AXES = ("lat", "row")
CHUNKS = 2
f32 = jnp.float32
bf16 = jnp.bfloat16


def bits_below(n):
    return [1 << k for k in range(n.bit_length() - 1)]


class Grid:
    def __init__(self, mesh):
        self.lats, self.rows = mesh.shape["lat"], mesh.shape["row"]
        self.size = self.lats * self.rows
        self.core = self.rows
        self.row_bits = bits_below(self.rows)
        self.chip_bits = [2 * self.rows * b for b in bits_below(self.lats // 2)]
        self.chips = self.lats // 2

    def stream_of(self, i):
        parity = (i // self.core) % 2
        for b in self.row_bits + self.chip_bits:
            parity = parity ^ ((i // b) % 2)
        return parity

    def orders(self, bits):
        return list(zip(bits, bits[::-1]))

    def swap_core(self, v):
        return lax.ppermute(v, AXES, [(i, i ^ self.core) for i in range(self.size)])

    def step(self, v, pair):
        target = [i ^ self.core ^ pair[self.stream_of(i)] for i in range(self.size)]
        return lax.ppermute(v, AXES, list(enumerate(target)))


def dot_rows(v, w):
    return lax.dot_general(v, w, (((1,), (1,)), ((), ())), preferred_element_type=f32)


def over_rows(u, v):
    return lax.dot_general(u, v, (((0,), (0,)), ((), ())), preferred_element_type=f32)


def on_device(grid, inputs, encoder, latent_bias, decoder, center_bias):
    me = lax.axis_index("lat") * grid.rows + lax.axis_index("row")
    core = (me // grid.core) % 2
    stream = grid.stream_of(me)
    chip = me // (2 * grid.core)
    width = encoder.shape[1]
    half, block = inputs.shape[0] // 2, 2 * inputs.shape[1]
    part = half // CHUNKS
    row_steps, chip_steps = grid.orders(grid.row_bits), grid.orders(grid.chip_bits)

    theirs = grid.swap_core(inputs).astype(f32) - grid.swap_core(center_bias)
    mine = inputs.astype(f32) - center_bias
    shifted = jnp.where(
        core == 0,
        jnp.concatenate([mine, theirs], axis=1),
        jnp.concatenate([theirs, mine], axis=1),
    )
    shifted = jnp.where(stream == 0, shifted[:half], shifted[half:])

    held, masks = [shifted.astype(bf16)], [0]
    for b, mask in list(zip(grid.chip_bits, bits_below(grid.chips)))[::-1]:
        held = held + [grid.step(u, (b, b)) for u in held]
        masks = masks + [m ^ mask for m in masks]
        if b == grid.chip_bits[-1]:
            held[-1], encoder, decoder, latent_bias = lax.optimization_barrier(
                (held[-1], encoder, decoder, latent_bias)
            )
    held = [u for _, u in sorted(zip(masks, held), key=lambda t: t[0])]
    for mask in bits_below(grid.chips):
        flip = (chip // mask) % 2 == 1
        held = [jnp.where(flip, held[k ^ mask], held[k]) for k in range(len(held))]
    blocks = jnp.concatenate(held, axis=1)

    encoders = [encoder, grid.swap_core(encoder)]
    decoders = [decoder, grid.swap_core(decoder)]
    biases = [latent_bias, grid.swap_core(latent_bias)]

    def gather_rows(v):
        for pair in row_steps[:-1]:
            v = jnp.concatenate([v, grid.step(v, pair)], axis=0)
        return v, grid.step(v, row_steps[-1])

    parts = [slice(k * part, (k + 1) * part) for k in range(CHUNKS)]
    centered = [gather_rows(blocks[rows]) for rows in parts]

    latents, sigs, keeps, sends = [], [], [], []

    def forward(x):
        scaled = [4.0 * (dot_rows(x, e) + b) for e, b in zip(encoders, biases)]
        sigs.append([jax.nn.sigmoid(v) for v in scaled])
        latents.append([(jax.nn.softplus(v) / 4.0).astype(bf16) for v in scaled])
        return sum(jnp.dot(l, d, preferred_element_type=f32) for l, d in zip(latents[-1], decoders))

    for near, far in centered:
        if sends:
            sends[-1], far = lax.optimization_barrier((sends[-1], far))
        keeps.append(forward(near))
        sends.append(forward(far).astype(bf16))
    norms = [jnp.sqrt(jnp.sum(jnp.square(d.astype(f32)), axis=1) + 1e-06) for d in decoders]

    def placed(rows):
        zeros = jnp.zeros((part, block), f32)
        return jnp.concatenate(
            [jnp.where(chip == p, shifted[rows], zeros) for p in range(grid.chips)], axis=1
        )

    for i in range(len(row_steps))[::-1]:
        received = [grid.step(v, row_steps[i]) for v in sends]
        for k in range(CHUNKS):
            v = keeps[k] + received[k].astype(f32)
            n = v.shape[0] // 2
            if i > 0:
                keeps[k], sends[k] = v[:n], v[n:].astype(bf16)
            else:
                keeps[k] = v - placed(parts[k])
                sends[k] = keeps[k].astype(bf16)
    for pair in chip_steps:
        received = [grid.step(v, pair) for v in sends]
        for k in range(CHUNKS):
            keeps[k] = keeps[k] + received[k].astype(f32)
            sends[k] = keeps[k].astype(bf16)
    columns = sum(jnp.sum(v, axis=0, keepdims=True) for v in keeps)
    errors = [e for halves in [gather_rows(v) for v in sends] for e in halves]
    centered = [c for halves in centered for c in halves]

    pres = []
    for err, sig in zip(errors, sigs):
        grads = [dot_rows(err, d) + sparsity_weight * n for d, n in zip(decoders, norms)]
        pres.append([(g * v).astype(bf16) for g, v in zip(grads, sig)])
    centered, latents, errors, pres, columns = lax.optimization_barrier(
        (centered, latents, errors, pres, columns)
    )

    terms = (1.0 / grid.chips) * columns
    for side, enc in enumerate(encoders):
        bias = sum(jnp.sum(p[side].astype(f32), axis=0, keepdims=True) for p in pres)
        digits = []
        for _ in range(3):
            digits.append(lax.reduce_precision(bias, 8, 7))
            bias = bias - digits[-1]
        digits = jnp.concatenate(digits, axis=0).astype(bf16)
        products = jnp.dot(digits, enc, preferred_element_type=f32)
        terms = terms - jnp.sum(products, axis=0, keepdims=True)
    left = terms + grid.swap_core(terms)

    def halve(left, b):
        n = left.shape[1] // 2
        upper = (me // b) % 2 == 1
        kept = jnp.where(upper, left[:, n:], left[:, :n])
        sent = jnp.where(upper, left[:, :n], left[:, n:])
        return kept + grid.step(sent, (b, b))

    def all_rows(mine, theirs):
        return jnp.concatenate([*mine, grid.swap_core(jnp.concatenate(theirs, axis=0))], axis=0)

    pres = all_rows([p[0] for p in pres], [p[1] for p in pres])
    errors = all_rows(errors, errors)
    left, latents, centered = lax.optimization_barrier((left, latents, centered))
    latents = all_rows([l[0] for l in latents], [l[1] for l in latents])
    centered = all_rows(centered, centered)

    for k, b in enumerate((grid.row_bits + grid.chip_bits)[::-1]):
        if k == len(grid.chip_bits):
            left = left.reshape(2, width // grid.chips // 2)
        if k == 2:
            left, decoder_grad = lax.optimization_barrier((left, decoder_grad))
        if k == 3:
            left, encoder_grad = lax.optimization_barrier((left, encoder_grad))
        left = halve(left, b)
        if k == 0:
            left, latents, errors = lax.optimization_barrier((left, latents, errors))
            latent_total = jnp.sum(latents.astype(f32), axis=0)
            scale = (sparsity_weight * latent_total / norms[0])[:, None]
            decoder_grad = over_rows(latents, errors) + scale * decoder.astype(f32)
            decoder_grad = decoder_grad.astype(bf16)
        if k == 1:
            left, pres, centered = lax.optimization_barrier((left, pres, centered))
            bias_grad = jnp.sum(pres.astype(f32), axis=0)
            encoder_grad = over_rows(pres, centered).astype(bf16)
    center_grad = jnp.where(core == 0, left[0], left[1])
    return (encoder_grad, decoder_grad, bias_grad, center_grad)


def solution(mesh):
    grid = Grid(mesh)
    in_specs = (P("row", "lat"), P(AXES, None), P(AXES), P(AXES, None), P("lat"))
    out_specs = (P(AXES, None), P(AXES, None), P(AXES), P(AXES))

    def device_function(*args):
        return on_device(grid, *args)

    return jax.shard_map(
        device_function, mesh=mesh, in_specs=in_specs, out_specs=out_specs, check_vma=False
    )
```

```python
import jax
import jax.numpy as jnp
from jax import lax
from jax.sharding import PartitionSpec as P

sparsity_weight = 1.0
AXES = ("lat", "row")
CHUNKS = 2
f32 = jnp.float32
bf16 = jnp.bfloat16


def bits_below(n):
    return [1 << k for k in range(n.bit_length() - 1)]


class Grid:
    def __init__(self, mesh):
        self.lats, self.rows = mesh.shape["lat"], mesh.shape["row"]
        self.size = self.lats * self.rows
        self.core = self.rows
        self.row_bits = bits_below(self.rows)
        self.chip_bits = [2 * self.rows * b for b in bits_below(self.lats // 2)]
        self.chips = self.lats // 2

    def stream_of(self, i):
        parity = (i // self.core) % 2
        for b in self.row_bits + self.chip_bits:
            parity = parity ^ ((i // b) % 2)
        return parity

    def orders(self, bits):
        return list(zip(bits, bits[::-1]))

    def swap_core(self, v):
        return lax.ppermute(v, AXES, [(i, i ^ self.core) for i in range(self.size)])

    def step(self, v, pair):
        target = [i ^ self.core ^ pair[self.stream_of(i)] for i in range(self.size)]
        return lax.ppermute(v, AXES, list(enumerate(target)))

    def from_chip(self, v, mask):
        across = mask * 2 * self.rows
        if bin(mask).count("1") % 2:
            return self.step(v, (across, across))
        return lax.ppermute(v, AXES, [(i, i ^ across) for i in range(self.size)])


def after(v, *others):
    return lax.optimization_barrier((v, *others))[0]


def dot_rows(v, w):
    return lax.dot_general(v, w, (((1,), (1,)), ((), ())), preferred_element_type=f32)


def over_rows(u, v):
    return lax.dot_general(u, v, (((0,), (0,)), ((), ())), preferred_element_type=f32)


def on_device(grid, inputs, encoder, latent_bias, decoder, center_bias):
    me = lax.axis_index("lat") * grid.rows + lax.axis_index("row")
    core = (me // grid.core) % 2
    stream = grid.stream_of(me)
    chip = me // (2 * grid.core)
    width = encoder.shape[1]
    half, block = inputs.shape[0] // 2, 2 * inputs.shape[1]
    part = half // CHUNKS
    row_steps, chip_steps = grid.orders(grid.row_bits), grid.orders(grid.chip_bits)

    theirs = grid.swap_core(inputs).astype(f32) - grid.swap_core(center_bias)
    mine = inputs.astype(f32) - center_bias
    shifted = jnp.where(
        core == 0,
        jnp.concatenate([mine, theirs], axis=1),
        jnp.concatenate([theirs, mine], axis=1),
    )
    shifted = jnp.where(stream == 0, shifted[:half], shifted[half:])

    held = {0: shifted.astype(bf16)}
    for mask in range(1, grid.chips)[::-1]:
        held[mask] = grid.from_chip(held[0], mask)
    held = [held[mask] for mask in range(grid.chips)]
    encoder, decoder, latent_bias = (after(w, held[-1]) for w in (encoder, decoder, latent_bias))
    for mask in bits_below(grid.chips):
        flip = (chip // mask) % 2 == 1
        held = [jnp.where(flip, held[k ^ mask], held[k]) for k in range(len(held))]
    blocks = jnp.concatenate(held, axis=1)

    encoders = [encoder, grid.swap_core(encoder)]
    decoders = [decoder, grid.swap_core(decoder)]
    biases = [latent_bias, grid.swap_core(latent_bias)]

    def gather_rows(v):
        for pair in row_steps[:-1]:
            v = jnp.concatenate([v, grid.step(v, pair)], axis=0)
        return v, grid.step(v, row_steps[-1])

    parts = [slice(k * part, (k + 1) * part) for k in range(CHUNKS)]
    centered = [gather_rows(blocks[rows]) for rows in parts]

    latents, sigs, keeps, sends = [], [], [], []

    def forward(x):
        scaled = [4.0 * (dot_rows(x, e) + b) for e, b in zip(encoders, biases)]
        sigs.append([jax.nn.sigmoid(v) for v in scaled])
        latents.append([(jax.nn.softplus(v) / 4.0).astype(bf16) for v in scaled])
        return sum(jnp.dot(l, d, preferred_element_type=f32) for l, d in zip(latents[-1], decoders))

    for near, far in centered:
        if sends:
            far = after(far, sends[-1])
        keeps.append(forward(near))
        sends.append(forward(far).astype(bf16))
    norms = [jnp.sqrt(jnp.sum(jnp.square(d.astype(f32)), axis=1) + 1e-06) for d in decoders]

    def placed(rows):
        zeros = jnp.zeros((part, block), f32)
        return jnp.concatenate(
            [jnp.where(chip == p, shifted[rows], zeros) for p in range(grid.chips)], axis=1
        )

    for i in range(len(row_steps))[::-1]:
        received = [grid.step(v, row_steps[i]) for v in sends]
        for k in range(CHUNKS):
            if k > 0:
                received[k] = after(received[k], sends[k - 1])
            v = keeps[k] + received[k].astype(f32)
            n = v.shape[0] // 2
            if i > 0:
                keeps[k], sends[k] = v[:n], v[n:].astype(bf16)
            else:
                keeps[k] = v - placed(parts[k])
                sends[k] = keeps[k].astype(bf16)
    for pair in chip_steps:
        received = [grid.step(v, pair) for v in sends]
        for k in range(CHUNKS):
            if k > 0:
                received[k] = after(received[k], sends[k - 1])
            keeps[k] = keeps[k] + received[k].astype(f32)
            sends[k] = keeps[k].astype(bf16)
    columns = sum(jnp.sum(v, axis=0, keepdims=True) for v in keeps)
    errors = [e for halves in [gather_rows(v) for v in sends] for e in halves]
    centered = [c for halves in centered for c in halves]

    pres = []
    for err, sig in zip(errors, sigs):
        grads = [dot_rows(err, d) + sparsity_weight * n for d, n in zip(decoders, norms)]
        pres.append([(g * v).astype(bf16) for g, v in zip(grads, sig)])
    centered, latents, errors, pres, columns = lax.optimization_barrier(
        (centered, latents, errors, pres, columns)
    )

    terms = (1.0 / grid.chips) * columns
    for side, enc in enumerate(encoders):
        bias = sum(jnp.sum(p[side].astype(f32), axis=0, keepdims=True) for p in pres)
        digits = []
        for _ in range(3):
            digits.append(lax.reduce_precision(bias, 8, 7))
            bias = bias - digits[-1]
        digits = jnp.concatenate(digits, axis=0).astype(bf16)
        products = jnp.dot(digits, enc, preferred_element_type=f32)
        terms = terms - jnp.sum(products, axis=0, keepdims=True)
    left = terms + grid.swap_core(terms)

    def halve(left, b):
        n = left.shape[1] // 2
        upper = (me // b) % 2 == 1
        kept = jnp.where(upper, left[:, n:], left[:, :n])
        sent = jnp.where(upper, left[:, :n], left[:, n:])
        return kept + grid.step(sent, (b, b))

    def all_rows(mine, theirs):
        return jnp.concatenate([*mine, grid.swap_core(jnp.concatenate(theirs, axis=0))], axis=0)

    pres = all_rows([p[0] for p in pres], [p[1] for p in pres])
    errors = all_rows(errors, errors)
    left, latents, centered = lax.optimization_barrier((left, latents, centered))
    latents = all_rows([l[0] for l in latents], [l[1] for l in latents])
    centered = all_rows(centered, centered)

    for k, b in enumerate((grid.row_bits + grid.chip_bits)[::-1]):
        if k == len(grid.chip_bits):
            left = left.reshape(2, width // grid.chips // 2)
        if k == 2:
            left, decoder_grad = lax.optimization_barrier((left, decoder_grad))
        if k == 3:
            left, encoder_grad = lax.optimization_barrier((left, encoder_grad))
        left = halve(left, b)
        if k == 0:
            left, latents, errors = lax.optimization_barrier((left, latents, errors))
            latent_total = jnp.sum(latents.astype(f32), axis=0)
            scale = (sparsity_weight * latent_total / norms[0])[:, None]
            decoder_grad = over_rows(latents, errors) + scale * decoder.astype(f32)
            decoder_grad = decoder_grad.astype(bf16)
        if k == 1:
            left, pres, centered = lax.optimization_barrier((left, pres, centered))
            bias_grad = jnp.sum(pres.astype(f32), axis=0)
            encoder_grad = over_rows(pres, centered).astype(bf16)
    center_grad = jnp.where(core == 0, left[0], left[1])
    return (encoder_grad, decoder_grad, bias_grad, center_grad)


def solution(mesh):
    grid = Grid(mesh)
    in_specs = (P("row", "lat"), P(AXES, None), P(AXES), P(AXES, None), P("lat"))
    out_specs = (P(AXES, None), P(AXES, None), P(AXES), P(AXES))

    def device_function(*args):
        return on_device(grid, *args)

    return jax.shard_map(
        device_function, mesh=mesh, in_specs=in_specs, out_specs=out_specs, check_vma=False
    )
```

```python
import jax
import jax.numpy as jnp
from jax import lax
from jax.sharding import PartitionSpec as P

sparsity_weight = 1.0
AXES = ("lat", "row")
CHUNKS = 2
f32 = jnp.float32
bf16 = jnp.bfloat16


def bits_below(n):
    return [1 << k for k in range(n.bit_length() - 1)]


class Grid:
    def __init__(self, mesh):
        self.lats, self.rows = mesh.shape["lat"], mesh.shape["row"]
        self.size = self.lats * self.rows
        self.core = self.rows
        self.row_bits = bits_below(self.rows)
        self.chip_bits = [2 * self.rows * b for b in bits_below(self.lats // 2)]
        self.chips = self.lats // 2

    def stream_of(self, i):
        parity = (i // self.core) % 2
        for b in self.row_bits + self.chip_bits:
            parity = parity ^ ((i // b) % 2)
        return parity

    def orders(self, bits):
        return list(zip(bits, bits[::-1]))

    def swap_core(self, v):
        return lax.ppermute(v, AXES, [(i, i ^ self.core) for i in range(self.size)])

    def step(self, v, pair):
        target = [i ^ self.core ^ pair[self.stream_of(i)] for i in range(self.size)]
        return lax.ppermute(v, AXES, list(enumerate(target)))

    def from_chip(self, v, mask):
        across = mask * 2 * self.rows
        if bin(mask).count("1") % 2:
            return self.step(v, (across, across))
        return lax.ppermute(v, AXES, [(i, i ^ across) for i in range(self.size)])


def after(v, *others):
    return lax.optimization_barrier((v, *others))[0]


def dot_rows(v, w):
    return lax.dot_general(v, w, (((1,), (1,)), ((), ())), preferred_element_type=f32)


def over_rows(u, v):
    return lax.dot_general(u, v, (((0,), (0,)), ((), ())), preferred_element_type=f32)


def on_device(grid, inputs, encoder, latent_bias, decoder, center_bias):
    me = lax.axis_index("lat") * grid.rows + lax.axis_index("row")
    core = (me // grid.core) % 2
    stream = grid.stream_of(me)
    chip = me // (2 * grid.core)
    width = encoder.shape[1]
    half, block = inputs.shape[0] // 2, 2 * inputs.shape[1]
    part = half // CHUNKS
    row_steps, chip_steps = grid.orders(grid.row_bits)[::-1], grid.orders(grid.chip_bits)
    chip_steps = [chip_steps[::-1] if k % 2 == 0 else chip_steps for k in range(CHUNKS)]

    theirs = grid.swap_core(inputs).astype(f32) - grid.swap_core(center_bias)
    mine = inputs.astype(f32) - center_bias
    shifted = jnp.where(
        core == 0,
        jnp.concatenate([mine, theirs], axis=1),
        jnp.concatenate([theirs, mine], axis=1),
    )
    shifted = jnp.where(stream == 0, shifted[:half], shifted[half:])

    held = {0: shifted.astype(bf16)}
    for mask in [grid.chips - 1, *range(1, grid.chips - 1)]:
        held[mask] = grid.from_chip(held[0], mask)
    held = [held[mask] for mask in range(grid.chips)]
    encoder, decoder, latent_bias = (after(w, held[-1]) for w in (encoder, decoder, latent_bias))
    for mask in bits_below(grid.chips):
        flip = (chip // mask) % 2 == 1
        held = [jnp.where(flip, held[k ^ mask], held[k]) for k in range(len(held))]
    blocks = jnp.concatenate(held, axis=1)

    encoders = [encoder, grid.swap_core(encoder)]
    decoders = [decoder, grid.swap_core(after(decoder, held[1]))]
    biases = [latent_bias, grid.swap_core(latent_bias)]

    def gather_rows(v):
        for pair in row_steps[:-1]:
            v = jnp.concatenate([v, grid.step(v, pair)], axis=0)
        return v, grid.step(v, row_steps[-1])

    parts = [slice(k * part, (k + 1) * part) for k in range(CHUNKS)]
    centered = [gather_rows(blocks[rows]) for rows in parts]

    latents, sigs, keeps, sends = [], [], [], []

    def forward(x):
        scaled = [4.0 * (dot_rows(x, e) + b) for e, b in zip(encoders, biases)]
        sigs.append([jax.nn.sigmoid(v) for v in scaled])
        latents.append([(jax.nn.softplus(v) / 4.0).astype(bf16) for v in scaled])
        return sum(jnp.dot(l, d, preferred_element_type=f32) for l, d in zip(latents[-1], decoders))

    centered[0] = (centered[0][0], after(centered[0][1], centered[-1][0]))
    for near, far in centered:
        if sends:
            far = after(far, sends[-1])
        keeps.append(forward(near))
        sends.append(forward(far).astype(bf16))
    norms = [jnp.sqrt(jnp.sum(jnp.square(d.astype(f32)), axis=1) + 1e-06) for d in decoders]

    def placed(rows):
        zeros = jnp.zeros((part, block), f32)
        return jnp.concatenate(
            [jnp.where(chip == p, shifted[rows], zeros) for p in range(grid.chips)], axis=1
        )

    for i in range(len(row_steps))[::-1]:
        received = [grid.step(v, row_steps[i]) for v in sends]
        for k in range(CHUNKS):
            v = keeps[k] + received[k].astype(f32)
            n = v.shape[0] // 2
            if i > 0:
                keeps[k], sends[k] = v[:n], v[n:].astype(bf16)
            else:
                keeps[k] = v - placed(parts[k])
                sends[k] = keeps[k].astype(bf16)
    for pairs in zip(*chip_steps):
        received = [grid.step(v, pair) for v, pair in zip(sends, pairs)]
        for k in range(CHUNKS):
            keeps[k] = keeps[k] + received[k].astype(f32)
            sends[k] = keeps[k].astype(bf16)
    columns = sum(jnp.sum(v, axis=0, keepdims=True) for v in keeps)
    errors = [e for halves in [gather_rows(v) for v in sends] for e in halves]
    centered = [c for halves in centered for c in halves]

    pres = []
    for err, sig in zip(errors, sigs):
        grads = [dot_rows(err, d) + sparsity_weight * n for d, n in zip(decoders, norms)]
        pres.append([(g * v).astype(bf16) for g, v in zip(grads, sig)])
    centered, latents, errors, pres, columns = lax.optimization_barrier(
        (centered, latents, errors, pres, columns)
    )

    terms = (1.0 / grid.chips) * columns
    for side, enc in enumerate(encoders):
        bias = sum(jnp.sum(p[side].astype(f32), axis=0, keepdims=True) for p in pres)
        digits = []
        for _ in range(3):
            digits.append(lax.reduce_precision(bias, 8, 7))
            bias = bias - digits[-1]
        digits = jnp.concatenate(digits, axis=0).astype(bf16)
        products = jnp.dot(digits, enc, preferred_element_type=f32)
        terms = terms - jnp.sum(products, axis=0, keepdims=True)
    left = terms + grid.swap_core(terms)

    def halve(left, b):
        n = left.shape[1] // 2
        upper = (me // b) % 2 == 1
        kept = jnp.where(upper, left[:, n:], left[:, :n])
        sent = jnp.where(upper, left[:, :n], left[:, n:])
        return kept + grid.step(sent, (b, b))

    def all_rows(mine, theirs):
        return jnp.concatenate([*mine, grid.swap_core(jnp.concatenate(theirs, axis=0))], axis=0)

    pres = all_rows([p[0] for p in pres], [p[1] for p in pres])
    errors = all_rows(errors, errors)
    left, latents, centered = lax.optimization_barrier((left, latents, centered))
    latents = all_rows([l[0] for l in latents], [l[1] for l in latents])
    centered = all_rows(centered, centered)

    for k, b in enumerate((grid.row_bits + grid.chip_bits)[::-1]):
        if k == len(grid.chip_bits):
            left = left.reshape(2, width // grid.chips // 2)
        if k == 2:
            left, decoder_grad = lax.optimization_barrier((left, decoder_grad))
        if k == 3:
            left, encoder_grad = lax.optimization_barrier((left, encoder_grad))
        left = halve(left, b)
        if k == 0:
            left, latents, errors = lax.optimization_barrier((left, latents, errors))
            latent_total = jnp.sum(latents.astype(f32), axis=0)
            scale = (sparsity_weight * latent_total / norms[0])[:, None]
            decoder_grad = over_rows(latents, errors) + scale * decoder.astype(f32)
            decoder_grad = decoder_grad.astype(bf16)
        if k == 1:
            left, pres, centered = lax.optimization_barrier((left, pres, centered))
            bias_grad = jnp.sum(pres.astype(f32), axis=0)
            encoder_grad = over_rows(pres, centered).astype(bf16)
    center_grad = jnp.where(core == 0, left[0], left[1])
    return (encoder_grad, decoder_grad, bias_grad, center_grad)


def solution(mesh):
    grid = Grid(mesh)
    in_specs = (P("row", "lat"), P(AXES, None), P(AXES), P(AXES, None), P("lat"))
    out_specs = (P(AXES, None), P(AXES, None), P(AXES), P(AXES))

    def device_function(*args):
        return on_device(grid, *args)

    return jax.shard_map(
        device_function, mesh=mesh, in_specs=in_specs, out_specs=out_specs, check_vma=False
    )
```

```python
import jax
import jax.numpy as jnp
from jax import lax
from jax.sharding import PartitionSpec as P

sparsity_weight = 1.0
AXES = ("lat", "row")
CHUNKS = 2
f32 = jnp.float32
bf16 = jnp.bfloat16


def bits_below(n):
    return [1 << k for k in range(n.bit_length() - 1)]


class Grid:
    def __init__(self, mesh):
        self.lats, self.rows = mesh.shape["lat"], mesh.shape["row"]
        self.size = self.lats * self.rows
        self.core = self.rows
        self.row_bits = bits_below(self.rows)
        self.chip_bits = [2 * self.rows * b for b in bits_below(self.lats // 2)]
        self.chips = self.lats // 2

    def stream_of(self, i):
        parity = (i // self.core) % 2
        for b in self.row_bits + self.chip_bits:
            parity = parity ^ ((i // b) % 2)
        return parity

    def orders(self, bits):
        return list(zip(bits, bits[::-1]))

    def swap_core(self, v):
        return lax.ppermute(v, AXES, [(i, i ^ self.core) for i in range(self.size)])

    def step(self, v, pair):
        target = [i ^ self.core ^ pair[self.stream_of(i)] for i in range(self.size)]
        return lax.ppermute(v, AXES, list(enumerate(target)))

    def from_chip(self, v, mask):
        across = mask * 2 * self.rows
        if bin(mask).count("1") % 2:
            return self.step(v, (across, across))
        return lax.ppermute(v, AXES, [(i, i ^ across) for i in range(self.size)])


def after(v, *others):
    return lax.optimization_barrier((v, *others))[0]


def dot_rows(v, w):
    return lax.dot_general(v, w, (((1,), (1,)), ((), ())), preferred_element_type=f32)


def over_rows(u, v):
    return lax.dot_general(u, v, (((0,), (0,)), ((), ())), preferred_element_type=f32)


def on_device(grid, inputs, encoder, latent_bias, decoder, center_bias):
    me = lax.axis_index("lat") * grid.rows + lax.axis_index("row")
    core = (me // grid.core) % 2
    stream = grid.stream_of(me)
    chip = me // (2 * grid.core)
    width = encoder.shape[1]
    half, block = inputs.shape[0] // 2, 2 * inputs.shape[1]
    part = half // CHUNKS
    row_steps, chip_steps = grid.orders(grid.row_bits)[::-1], grid.orders(grid.chip_bits)
    chip_steps = [chip_steps[::-1] if k % 2 == 0 else chip_steps for k in range(CHUNKS)]

    theirs = grid.swap_core(inputs).astype(f32) - grid.swap_core(center_bias)
    mine = inputs.astype(f32) - center_bias
    shifted = jnp.where(
        core == 0,
        jnp.concatenate([mine, theirs], axis=1),
        jnp.concatenate([theirs, mine], axis=1),
    )
    shifted = jnp.where(stream == 0, shifted[:half], shifted[half:])

    held = {0: shifted.astype(bf16)}
    for mask in [grid.chips - 1, *range(1, grid.chips - 1)]:
        held[mask] = grid.from_chip(held[0], mask)
    held = [held[mask] for mask in range(grid.chips)]
    encoder, decoder, latent_bias = (after(w, held[-1]) for w in (encoder, decoder, latent_bias))
    for mask in bits_below(grid.chips):
        flip = (chip // mask) % 2 == 1
        held = [jnp.where(flip, held[k ^ mask], held[k]) for k in range(len(held))]
    blocks = jnp.concatenate(held, axis=1)

    encoders = [encoder, grid.swap_core(encoder)]
    decoders = [decoder, grid.swap_core(after(decoder, held[1]))]
    biases = [latent_bias, grid.swap_core(latent_bias)]

    def gather_rows(v):
        for pair in row_steps[:-1]:
            v = jnp.concatenate([v, grid.step(v, pair)], axis=0)
        return v, grid.step(v, row_steps[-1])

    parts = [slice(k * part, (k + 1) * part) for k in range(CHUNKS)]
    centered = [gather_rows(blocks[rows]) for rows in parts]

    latents, sigs, keeps, sends = [], [], [], []

    def forward(x):
        scaled = [4.0 * (dot_rows(x, e) + b) for e, b in zip(encoders, biases)]
        sigs.append([jax.nn.sigmoid(v) for v in scaled])
        latents.append([(jax.nn.softplus(v) / 4.0).astype(bf16) for v in scaled])
        return sum(jnp.dot(l, d, preferred_element_type=f32) for l, d in zip(latents[-1], decoders))

    centered[0] = (centered[0][0], after(centered[0][1], centered[-1][0]))
    for near, far in centered:
        if sends:
            far = after(far, sends[-1])
        keeps.append(forward(near))
        sends.append(forward(far).astype(bf16))
    norms = [jnp.sqrt(jnp.sum(jnp.square(d.astype(f32)), axis=1) + 1e-06) for d in decoders]

    def placed(rows):
        zeros = jnp.zeros((part, block), f32)
        return jnp.concatenate(
            [jnp.where(chip == p, shifted[rows], zeros) for p in range(grid.chips)], axis=1
        )

    for i in range(len(row_steps))[::-1]:
        received = [grid.step(v, row_steps[i]) for v in sends]
        for k in range(CHUNKS):
            v = keeps[k] + received[k].astype(f32)
            n = v.shape[0] // 2
            if i > 0:
                keeps[k], sends[k] = v[:n], v[n:].astype(bf16)
            else:
                keeps[k] = v - placed(parts[k])
                sends[k] = keeps[k].astype(bf16)
    for pairs in zip(*chip_steps):
        received = [grid.step(v, pair) for v, pair in zip(sends, pairs)]
        for k in range(CHUNKS):
            keeps[k] = keeps[k] + received[k].astype(f32)
            sends[k] = keeps[k].astype(bf16)
    columns = sum(jnp.sum(v, axis=0, keepdims=True) for v in keeps)
    errors = [e for halves in [gather_rows(v) for v in sends] for e in halves]
    centered = [c for halves in centered for c in halves]

    errors[0] = after(errors[0], sends[-1])
    pres = []
    for err, sig in zip(errors, sigs):
        grads = [dot_rows(err, d) + sparsity_weight * n for d, n in zip(decoders, norms)]
        pres.append([(g * v).astype(bf16) for g, v in zip(grads, sig)])
    centered, latents, errors, pres, columns = lax.optimization_barrier(
        (centered, latents, errors, pres, columns)
    )

    terms = (1.0 / grid.chips) * columns
    for side, enc in enumerate(encoders):
        bias = sum(jnp.sum(p[side].astype(f32), axis=0, keepdims=True) for p in pres)
        digits = []
        for _ in range(3):
            digits.append(lax.reduce_precision(bias, 8, 7))
            bias = bias - digits[-1]
        digits = jnp.concatenate(digits, axis=0).astype(bf16)
        products = jnp.dot(digits, enc, preferred_element_type=f32)
        terms = terms - jnp.sum(products, axis=0, keepdims=True)
    left = terms + grid.swap_core(terms)

    def halve(left, b):
        n = left.shape[1] // 2
        upper = (me // b) % 2 == 1
        kept = jnp.where(upper, left[:, n:], left[:, :n])
        sent = jnp.where(upper, left[:, :n], left[:, n:])
        return kept + grid.step(sent, (b, b))

    def all_rows(mine, theirs):
        return jnp.concatenate([*mine, grid.swap_core(jnp.concatenate(theirs, axis=0))], axis=0)

    pres = all_rows([p[0] for p in pres], [p[1] for p in pres])
    errors = all_rows(errors, errors)
    left, latents, centered = lax.optimization_barrier((left, latents, centered))
    latents = all_rows([l[0] for l in latents], [l[1] for l in latents])
    centered = all_rows(centered, centered)

    for k, b in enumerate((grid.row_bits + grid.chip_bits)[::-1]):
        if k == len(grid.chip_bits):
            left = left.reshape(2, width // grid.chips // 2)
        if k == 2:
            left, decoder_grad = lax.optimization_barrier((left, decoder_grad))
        if k == 3:
            left, encoder_grad = lax.optimization_barrier((left, encoder_grad))
        left = halve(left, b)
        if k == 0:
            left, latents, errors = lax.optimization_barrier((left, latents, errors))
            latent_total = jnp.sum(latents.astype(f32), axis=0)
            scale = (sparsity_weight * latent_total / norms[0])[:, None]
            decoder_grad = over_rows(latents, errors) + scale * decoder.astype(f32)
            decoder_grad = decoder_grad.astype(bf16)
        if k == 1:
            left, pres, centered = lax.optimization_barrier((left, pres, centered))
            bias_grad = jnp.sum(pres.astype(f32), axis=0)
            encoder_grad = over_rows(pres, centered).astype(bf16)
    center_grad = jnp.where(core == 0, left[0], left[1])
    return (encoder_grad, decoder_grad, bias_grad, center_grad)


def solution(mesh):
    grid = Grid(mesh)
    in_specs = (P("row", "lat"), P(AXES, None), P(AXES), P(AXES, None), P("lat"))
    out_specs = (P(AXES, None), P(AXES, None), P(AXES), P(AXES))

    def device_function(*args):
        return on_device(grid, *args)

    return jax.shard_map(
        device_function, mesh=mesh, in_specs=in_specs, out_specs=out_specs, check_vma=False
    )
```

```python
import jax
import jax.numpy as jnp
from jax import lax
from jax.sharding import PartitionSpec as P

sparsity_weight = 1.0
AXES = ("lat", "row")
CHUNKS = 2
f32 = jnp.float32
bf16 = jnp.bfloat16


def bits_below(n):
    return [1 << k for k in range(n.bit_length() - 1)]


class Grid:
    def __init__(self, mesh):
        self.lats, self.rows = mesh.shape["lat"], mesh.shape["row"]
        self.size = self.lats * self.rows
        self.core = self.rows
        self.row_bits = bits_below(self.rows)
        self.chip_bits = [2 * self.rows * b for b in bits_below(self.lats // 2)]
        self.chips = self.lats // 2

    def stream_of(self, i):
        parity = (i // self.core) % 2
        for b in self.row_bits + self.chip_bits:
            parity = parity ^ ((i // b) % 2)
        return parity

    def orders(self, bits):
        return list(zip(bits, bits[::-1]))

    def swap_core(self, v):
        return lax.ppermute(v, AXES, [(i, i ^ self.core) for i in range(self.size)])

    def step(self, v, pair):
        target = [i ^ self.core ^ pair[self.stream_of(i)] for i in range(self.size)]
        return lax.ppermute(v, AXES, list(enumerate(target)))

    def from_chip(self, v, mask):
        across = mask * 2 * self.rows
        if bin(mask).count("1") % 2:
            return self.step(v, (across, across))
        return lax.ppermute(v, AXES, [(i, i ^ across) for i in range(self.size)])


def after(v, *others):
    return lax.optimization_barrier((v, *others))[0]


def dot_rows(v, w):
    return lax.dot_general(v, w, (((1,), (1,)), ((), ())), preferred_element_type=f32)


def over_rows(u, v):
    return lax.dot_general(u, v, (((0,), (0,)), ((), ())), preferred_element_type=f32)


def on_device(grid, inputs, encoder, latent_bias, decoder, center_bias):
    me = lax.axis_index("lat") * grid.rows + lax.axis_index("row")
    core = (me // grid.core) % 2
    stream = grid.stream_of(me)
    chip = me // (2 * grid.core)
    width = encoder.shape[1]
    half, block = inputs.shape[0] // 2, 2 * inputs.shape[1]
    part = half // CHUNKS
    row_steps, chip_steps = grid.orders(grid.row_bits)[::-1], grid.orders(grid.chip_bits)
    chip_steps = [chip_steps[::-1]] * CHUNKS

    theirs = grid.swap_core(inputs).astype(f32) - grid.swap_core(center_bias)
    mine = inputs.astype(f32) - center_bias
    shifted = jnp.where(
        core == 0,
        jnp.concatenate([mine, theirs], axis=1),
        jnp.concatenate([theirs, mine], axis=1),
    )
    shifted = jnp.where(stream == 0, shifted[:half], shifted[half:])

    held = {0: shifted.astype(bf16)}
    for mask in [grid.chips - 1, *range(1, grid.chips - 1)]:
        held[mask] = grid.from_chip(held[0], mask)
    held = [held[mask] for mask in range(grid.chips)]
    encoder, decoder, latent_bias = (after(w, held[-1]) for w in (encoder, decoder, latent_bias))
    for mask in bits_below(grid.chips):
        flip = (chip // mask) % 2 == 1
        held = [jnp.where(flip, held[k ^ mask], held[k]) for k in range(len(held))]
    blocks = jnp.concatenate(held, axis=1)

    encoders = [encoder, grid.swap_core(encoder)]
    decoders = [decoder, grid.swap_core(decoder)]
    biases = [latent_bias, grid.swap_core(latent_bias)]

    def gather_rows(v):
        for pair in row_steps[:-1]:
            v = jnp.concatenate([v, grid.step(v, pair)], axis=0)
        return v, grid.step(v, row_steps[-1])

    parts = [slice(k * part, (k + 1) * part) for k in range(CHUNKS)]
    centered = [gather_rows(blocks[rows]) for rows in parts]

    latents, sigs, keeps, sends = [], [], [], []

    def forward(x):
        scaled = [4.0 * (dot_rows(x, e) + b) for e, b in zip(encoders, biases)]
        sigs.append([jax.nn.sigmoid(v) for v in scaled])
        latents.append([(jax.nn.softplus(v) / 4.0).astype(bf16) for v in scaled])
        return sum(jnp.dot(l, d, preferred_element_type=f32) for l, d in zip(latents[-1], decoders))

    centered[0] = (centered[0][0], after(centered[0][1], centered[-1][0]))
    for near, far in centered:
        if sends:
            far = after(far, sends[-1])
        keeps.append(forward(near))
        sends.append(forward(far).astype(bf16))
    late = [decoders[0], after(decoders[1], keeps[-1])]
    norms = [jnp.sqrt(jnp.sum(jnp.square(d.astype(f32)), axis=1) + 1e-06) for d in late]

    def placed(rows):
        zeros = jnp.zeros((part, block), f32)
        return jnp.concatenate(
            [jnp.where(chip == p, shifted[rows], zeros) for p in range(grid.chips)], axis=1
        )

    for i in range(len(row_steps))[::-1]:
        received = [grid.step(v, row_steps[i]) for v in sends]
        for k in range(CHUNKS):
            if k > 0:
                received[k] = after(received[k], sends[k - 1])
            v = keeps[k] + received[k].astype(f32)
            n = v.shape[0] // 2
            if i > 0:
                keeps[k], sends[k] = v[:n], v[n:].astype(bf16)
            else:
                keeps[k] = v - placed(parts[k])
                sends[k] = keeps[k].astype(bf16)
    for pairs in zip(*chip_steps):
        received = [grid.step(v, pair) for v, pair in zip(sends, pairs)]
        for k in range(CHUNKS):
            if k > 0:
                received[k] = after(received[k], sends[k - 1])
            keeps[k] = keeps[k] + received[k].astype(f32)
            sends[k] = keeps[k].astype(bf16)
    columns = sum(jnp.sum(v, axis=0, keepdims=True) for v in keeps)
    errors = [e for halves in [gather_rows(v) for v in sends] for e in halves]
    centered = [c for halves in centered for c in halves]

    pres = []
    for err, sig in zip(errors, sigs):
        grads = [dot_rows(err, d) + sparsity_weight * n for d, n in zip(decoders, norms)]
        pres.append([(g * v).astype(bf16) for g, v in zip(grads, sig)])
    centered, latents, errors, pres, columns = lax.optimization_barrier(
        (centered, latents, errors, pres, columns)
    )

    terms = (1.0 / grid.chips) * columns
    for side, enc in enumerate(encoders):
        bias = sum(jnp.sum(p[side].astype(f32), axis=0, keepdims=True) for p in pres)
        digits = []
        for _ in range(3):
            digits.append(lax.reduce_precision(bias, 8, 7))
            bias = bias - digits[-1]
        digits = jnp.concatenate(digits, axis=0).astype(bf16)
        products = jnp.dot(digits, enc, preferred_element_type=f32)
        terms = terms - jnp.sum(products, axis=0, keepdims=True)
    left = terms + grid.swap_core(terms)

    def halve(left, b):
        n = left.shape[1] // 2
        upper = (me // b) % 2 == 1
        kept = jnp.where(upper, left[:, n:], left[:, :n])
        sent = jnp.where(upper, left[:, :n], left[:, n:])
        return kept + grid.step(sent, (b, b))

    def all_rows(mine, theirs):
        return jnp.concatenate([*mine, grid.swap_core(jnp.concatenate(theirs, axis=0))], axis=0)

    pres = all_rows([p[0] for p in pres], [p[1] for p in pres])
    errors = all_rows(errors, errors)
    left, latents, centered = lax.optimization_barrier((left, latents, centered))
    latents = all_rows([l[0] for l in latents], [l[1] for l in latents])
    centered = all_rows(centered, centered)

    for k, b in enumerate((grid.row_bits + grid.chip_bits)[::-1]):
        if k == len(grid.chip_bits):
            left = left.reshape(2, width // grid.chips // 2)
        if k == 2:
            left, decoder_grad = lax.optimization_barrier((left, decoder_grad))
        if k == 3:
            left, encoder_grad = lax.optimization_barrier((left, encoder_grad))
        left = halve(left, b)
        if k == 0:
            left, latents, errors = lax.optimization_barrier((left, latents, errors))
            latent_total = jnp.sum(latents.astype(f32), axis=0)
            scale = (sparsity_weight * latent_total / norms[0])[:, None]
            decoder_grad = over_rows(latents, errors) + scale * decoder.astype(f32)
            decoder_grad = decoder_grad.astype(bf16)
        if k == 1:
            left, pres, centered = lax.optimization_barrier((left, pres, centered))
            bias_grad = jnp.sum(pres.astype(f32), axis=0)
            encoder_grad = over_rows(pres, centered).astype(bf16)
    center_grad = jnp.where(core == 0, left[0], left[1])
    return (encoder_grad, decoder_grad, bias_grad, center_grad)


def solution(mesh):
    grid = Grid(mesh)
    in_specs = (P("row", "lat"), P(AXES, None), P(AXES), P(AXES, None), P("lat"))
    out_specs = (P(AXES, None), P(AXES, None), P(AXES), P(AXES))

    def device_function(*args):
        return on_device(grid, *args)

    return jax.shard_map(
        device_function, mesh=mesh, in_specs=in_specs, out_specs=out_specs, check_vma=False
    )
```

```python
import jax
import jax.numpy as jnp
from jax import lax
from jax.sharding import PartitionSpec as P

sparsity_weight = 1.0
AXES = ("lat", "row")
CHUNKS = 2
f32 = jnp.float32
bf16 = jnp.bfloat16


def bits_below(n):
    return [1 << k for k in range(n.bit_length() - 1)]


class Grid:
    def __init__(self, mesh):
        self.lats, self.rows = mesh.shape["lat"], mesh.shape["row"]
        self.size = self.lats * self.rows
        self.core = self.rows
        self.row_bits = bits_below(self.rows)
        self.chip_bits = [2 * self.rows * b for b in bits_below(self.lats // 2)]
        self.chips = self.lats // 2

    def stream_of(self, i):
        parity = (i // self.core) % 2
        for b in self.row_bits + self.chip_bits:
            parity = parity ^ ((i // b) % 2)
        return parity

    def orders(self, bits):
        return list(zip(bits, bits[::-1]))

    def swap_core(self, v):
        return lax.ppermute(v, AXES, [(i, i ^ self.core) for i in range(self.size)])

    def step(self, v, pair):
        target = [i ^ self.core ^ pair[self.stream_of(i)] for i in range(self.size)]
        return lax.ppermute(v, AXES, list(enumerate(target)))

    def from_chip(self, v, mask):
        across = mask * 2 * self.rows
        if bin(mask).count("1") % 2:
            return self.step(v, (across, across))
        return lax.ppermute(v, AXES, [(i, i ^ across) for i in range(self.size)])


def after(v, *others):
    return lax.optimization_barrier((v, *others))[0]


def dot_rows(v, w):
    return lax.dot_general(v, w, (((1,), (1,)), ((), ())), preferred_element_type=f32)


def over_rows(u, v):
    return lax.dot_general(u, v, (((0,), (0,)), ((), ())), preferred_element_type=f32)


def on_device(grid, inputs, encoder, latent_bias, decoder, center_bias):
    me = lax.axis_index("lat") * grid.rows + lax.axis_index("row")
    core = (me // grid.core) % 2
    stream = grid.stream_of(me)
    chip = me // (2 * grid.core)
    width = encoder.shape[1]
    half, block = inputs.shape[0] // 2, 2 * inputs.shape[1]
    part = half // CHUNKS
    row_steps, chip_steps = grid.orders(grid.row_bits)[::-1], grid.orders(grid.chip_bits)
    chip_steps = [chip_steps[::-1]] * CHUNKS

    theirs = grid.swap_core(inputs).astype(f32) - grid.swap_core(center_bias)
    mine = inputs.astype(f32) - center_bias
    shifted = jnp.where(
        core == 0,
        jnp.concatenate([mine, theirs], axis=1),
        jnp.concatenate([theirs, mine], axis=1),
    )
    shifted = jnp.where(stream == 0, shifted[:half], shifted[half:])

    held = {0: shifted.astype(bf16)}
    for mask in [grid.chips - 1, *range(1, grid.chips - 1)]:
        held[mask] = grid.from_chip(held[0], mask)
    held = [held[mask] for mask in range(grid.chips)]
    encoder, decoder, latent_bias = (after(w, held[-1]) for w in (encoder, decoder, latent_bias))
    for mask in bits_below(grid.chips):
        flip = (chip // mask) % 2 == 1
        held = [jnp.where(flip, held[k ^ mask], held[k]) for k in range(len(held))]
    blocks = jnp.concatenate(held, axis=1)

    encoders = [encoder, grid.swap_core(encoder)]
    decoders = [decoder, grid.swap_core(decoder)]
    biases = [latent_bias, grid.swap_core(latent_bias)]

    def gather_rows(v):
        for pair in row_steps[:-1]:
            v = jnp.concatenate([v, grid.step(v, pair)], axis=0)
        return v, grid.step(v, row_steps[-1])

    parts = [slice(k * part, (k + 1) * part) for k in range(CHUNKS)]
    centered = [gather_rows(blocks[rows]) for rows in parts]

    latents, sigs, keeps, sends = [], [], [], []

    def forward(x):
        scaled = [4.0 * (dot_rows(x, e) + b) for e, b in zip(encoders, biases)]
        sigs.append([jax.nn.sigmoid(v) for v in scaled])
        latents.append([(jax.nn.softplus(v) / 4.0).astype(bf16) for v in scaled])
        return sum(jnp.dot(l, d, preferred_element_type=f32) for l, d in zip(latents[-1], decoders))

    centered[0] = (centered[0][0], after(centered[0][1], centered[-1][0]))
    for near, far in centered:
        if sends:
            far = after(far, sends[-1])
        keeps.append(forward(near))
        sends.append(forward(far).astype(bf16))
    late = [decoders[0], after(decoders[1], keeps[-1])]
    norms = [jnp.sqrt(jnp.sum(jnp.square(d.astype(f32)), axis=1) + 1e-06) for d in late]

    def placed(rows):
        zeros = jnp.zeros((part, block), f32)
        return jnp.concatenate(
            [jnp.where(chip == p, shifted[rows], zeros) for p in range(grid.chips)], axis=1
        )

    for i in range(len(row_steps))[::-1]:
        received = [grid.step(v, row_steps[i]) for v in sends]
        for k in range(CHUNKS):
            if k > 0:
                received[k] = after(received[k], sends[k - 1])
            v = keeps[k] + received[k].astype(f32)
            n = v.shape[0] // 2
            if i > 0:
                keeps[k], sends[k] = v[:n], v[n:].astype(bf16)
            else:
                keeps[k] = v - placed(parts[k])
                sends[k] = keeps[k].astype(bf16)
    for pairs in zip(*chip_steps):
        received = [grid.step(v, pair) for v, pair in zip(sends, pairs)]
        for k in range(CHUNKS):
            if k > 0:
                received[k] = after(received[k], sends[k - 1])
            keeps[k] = keeps[k] + received[k].astype(f32)
            sends[k] = keeps[k].astype(bf16)
    columns = sum(jnp.sum(v, axis=0, keepdims=True) for v in keeps)
    errors = [e for halves in [gather_rows(v) for v in sends] for e in halves]
    centered = [c for halves in centered for c in halves]

    pres = []
    for err, sig in zip(errors, sigs):
        grads = [dot_rows(err, d) + sparsity_weight * n for d, n in zip(decoders, norms)]
        pres.append([(g * v).astype(bf16) for g, v in zip(grads, sig)])
    centered, latents, errors, pres, columns = lax.optimization_barrier(
        (centered, latents, errors, pres, columns)
    )

    terms = (1.0 / grid.chips) * columns
    for side, enc in enumerate(encoders):
        bias = sum(jnp.sum(p[side].astype(f32), axis=0, keepdims=True) for p in pres)
        digits = []
        for _ in range(3):
            digits.append(lax.reduce_precision(bias, 8, 7))
            bias = bias - digits[-1]
        digits = jnp.concatenate(digits, axis=0).astype(bf16)
        products = jnp.dot(digits, enc, preferred_element_type=f32)
        terms = terms - jnp.sum(products, axis=0, keepdims=True)
    left = terms + grid.swap_core(terms)

    def halve(left, b):
        n = left.shape[1] // 2
        upper = (me // b) % 2 == 1
        kept = jnp.where(upper, left[:, n:], left[:, :n])
        sent = jnp.where(upper, left[:, :n], left[:, n:])
        return kept + grid.step(sent, (b, b))

    def all_rows(mine, theirs):
        return jnp.concatenate([*mine, grid.swap_core(jnp.concatenate(theirs, axis=0))], axis=0)

    latents = all_rows([l[0] for l in latents], [l[1] for l in latents])
    errors = all_rows(errors, errors)
    left, pres, centered = lax.optimization_barrier((left, pres, centered))
    pres = all_rows([p[0] for p in pres], [p[1] for p in pres])
    centered = all_rows(centered, centered)

    for k, b in enumerate((grid.row_bits + grid.chip_bits)[::-1]):
        if k == len(grid.chip_bits):
            left = left.reshape(2, width // grid.chips // 2)
        if k == 2:
            left, decoder_grad = lax.optimization_barrier((left, decoder_grad))
        if k == 3:
            left, encoder_grad = lax.optimization_barrier((left, encoder_grad))
        left = halve(left, b)
        if k == 0:
            left, latents, errors = lax.optimization_barrier((left, latents, errors))
            latent_total = jnp.sum(latents.astype(f32), axis=0)
            scale = (sparsity_weight * latent_total / norms[0])[:, None]
            decoder_grad = over_rows(latents, errors) + scale * decoder.astype(f32)
            decoder_grad = decoder_grad.astype(bf16)
        if k == 1:
            left, pres, centered = lax.optimization_barrier((left, pres, centered))
            bias_grad = jnp.sum(pres.astype(f32), axis=0)
            encoder_grad = over_rows(pres, centered).astype(bf16)
    center_grad = jnp.where(core == 0, left[0], left[1])
    return (encoder_grad, decoder_grad, bias_grad, center_grad)


def solution(mesh):
    grid = Grid(mesh)
    in_specs = (P("row", "lat"), P(AXES, None), P(AXES), P(AXES, None), P("lat"))
    out_specs = (P(AXES, None), P(AXES, None), P(AXES), P(AXES))

    def device_function(*args):
        return on_device(grid, *args)

    return jax.shard_map(
        device_function, mesh=mesh, in_specs=in_specs, out_specs=out_specs, check_vma=False
    )
```
